32 devices in a mesh: mem: 4 (over x, core), gx: 4 (over z), gy: 2 (over y).
Axes of the slice: x: 2, y: 2, z: 4, core: 2. Of those that a mesh axis runs over, the one named last changes fastest.
Arguments:
- perturbations: float32 [4, 32, 128, 512], P('mem', None, 'gx', 'gy'), may hold values from -9 to 9
- control: float32 [32, 128, 512], P(None, 'gx', 'gy'), may hold values from -6 to 6
Outputs:
- increment: float32 [32, 128, 512], P('mem', 'gx', 'gy')
The draws below stay inside these ranges and needn't reach their ends.
All inputs are finite; a program needn't handle non-finite values.
Results may differ from the reference program's by a relative error of at most 0.0001.
Values sent between devices are 32-bit elements; how exact they have to be, the bound alone decides.
A program may use at most 64 MiB of HBM per device.

```python
import jax
import jax.numpy as jnp
from jax import lax

FIELDS = 32
MEMBERS = 4
NX = 128
NY = 512


def spiked(array, stream_key, source, target, blocks, factor):
    def block_of(position):
        return (jnp.arange(array.shape[position]) // (array.shape[position] // blocks)).reshape((-1,) + (1,) * (array.ndim - 1 - position))

    first = jax.random.permutation(stream_key, blocks)[block_of(target)]
    far = (block_of(target) + blocks // 2) % blocks
    return jnp.where((block_of(source) == first) | (block_of(source) == far), factor * array, array)


def levels(key, shape, pieces, low, top_value):
    loudness, own = 1.0, jax.random.fold_in(key, 6)
    for axis_at, blocks in pieces:
        heights = jnp.exp(jax.random.uniform(jax.random.fold_in(own, axis_at), (blocks,), jnp.float32, low / len(pieces), top_value / len(pieces)))
        loudness = loudness * jnp.repeat(heights, shape[axis_at] // blocks).reshape([-1 if axis == axis_at else 1 for axis in range(len(shape))])
    return loudness


def gaussian(key, shape, deviation, reach, pieces=(), dtype=jnp.bfloat16):
    drawn = jax.random.normal(key, shape, jnp.float32) * deviation
    if len(pieces) > 0:
        drawn = levels(key, shape, pieces, -0.22, 0.18) * drawn
    return jnp.clip(drawn, min=-reach, max=reach).astype(dtype)


def heavy_noise(key, dims, deviation, limit, pieces, heavy, kind=jnp.bfloat16):
    array = deviation * jax.random.normal(key, dims, jnp.float32)
    if pieces:
        array = array * levels(key, dims, pieces, -0.22, 0.18)
    return jnp.clip(spiked(array, jax.random.fold_in(key, 3), *heavy), -limit, limit).astype(kind)


def setup_inputs(seed: int = 0) -> dict:
    splits = jax.random.split(jax.random.key(seed), 3)
    return {
        "perturbations": heavy_noise(splits[0], (MEMBERS, FIELDS, NX, NY), 1.5, 9.0, ((0, 4), (2, 4), (3, 2)), (0, 1, 4, 2.0), jnp.float32),
        "control": gaussian(splits[1], (FIELDS, NX, NY), 1.0, 6.0, ((1, 4), (2, 2)), jnp.float32),
    }


def tap_weights():
    offsets = jnp.arange(-4, 5).astype(jnp.float32)
    raw_taps = jnp.exp(-offsets * offsets / 18.0)
    return raw_taps / jnp.sqrt(jnp.sum(raw_taps * raw_taps))

def smooth(values):
    weights = tap_weights()
    count_x, count_y = (values.shape[-2], values.shape[-1])
    widths = [(0, 0)] * (values.ndim - 2) + [(4, 4), (4, 4)]
    padded = jnp.pad(values, widths)
    along_x = sum((weights[offset] * padded[..., offset:offset + count_x, :] for offset in range(9)))
    return sum((weights[offset] * along_x[..., offset:offset + count_y] for offset in range(9)))

def restrict(values):
    shape_now = values.shape
    blocks = values.reshape(shape_now[:-2] + (shape_now[-2] // 2, 2, shape_now[-1] // 2, 2))
    return 0.5 * lax.optimization_barrier(jnp.sum(blocks, axis=(-3, -1)))

def prolong(coarse):
    return 0.5 * jnp.repeat(jnp.repeat(coarse, 2, axis=-2), 2, axis=-1)

def localize(values):
    return smooth(values) + prolong(smooth(restrict(values)))

def reference(perturbations, control):

    def add_member(running, member_field):
        alpha = localize(localize(member_field * control))
        return (running + member_field * alpha, None)
    running, unused = lax.scan(add_member, jnp.zeros(control.shape, jnp.float32), perturbations)
    return running / (MEMBERS - 1)
```

```python
import functools
import math

import jax
import jax.numpy as jnp
import ml_dtypes
import numpy as np
from jax import lax
from jax.experimental import pallas as pl
from jax.experimental.pallas import tpu as pltpu
from jax.sharding import PartitionSpec as P

MESH = pl.DeviceIdType.MESH
REACH = 16
GROUP = 8
LANES = 128


def smoothing(n):
    o = np.arange(-4, 5).astype(np.float64)
    taps = np.exp(-o * o / 18.0)
    taps = taps / np.sqrt(np.sum(taps * taps))
    a = np.zeros((n, n))
    for k, t in zip(range(-4, 5), taps):
        a += t * np.eye(n, k=k)
    return a


def four_terms(n):
    a = smoothing(n)
    r = np.kron(np.eye(n // 2), np.ones((1, 2))) / math.sqrt(2.0)
    b = r.T @ smoothing(n // 2) @ r
    return [a @ a, a @ b, b @ a, b @ b]


def split_np(m):
    hi = m.astype(np.float32).astype(ml_dtypes.bfloat16)
    lo = (m - hi.astype(np.float64)).astype(np.float32).astype(ml_dtypes.bfloat16)
    return hi, lo


def constants(nx, ny, gx, gy):
    rows, cols = nx // gx, ny // gy
    xs = []
    for g in range(gx):
        blocks = []
        for m in four_terms(nx):
            wide = np.pad(m, ((0, 0), (REACH, REACH)))
            blocks.append(wide[g * rows : (g + 1) * rows, g * rows : (g + 1) * rows + 2 * REACH])
        hi, lo = split_np(np.concatenate(blocks, 0))
        xs.append(np.concatenate([hi, lo, hi], 1))
    ys, hs = [], []
    for g in range(gy):
        own, edge = [], []
        for m in four_terms(ny):
            mine = m[g * cols : (g + 1) * cols]
            own.append(mine[:, g * cols : (g + 1) * cols].T)
            if g == 0:
                part = mine[cols - REACH :, cols : cols + REACH].T
            else:
                part = mine[:REACH, g * cols - REACH : g * cols].T
            block = np.zeros((LANES, LANES))
            for s in range(GROUP):
                before = (s + GROUP - 1) % GROUP
                slot_in, slot_out = (s, before) if g == 0 else (before, s)
                block[slot_in * REACH :][:REACH, slot_out * REACH : (slot_out + 1) * REACH] = part
            edge.append(block)
        ys.append(np.stack(split_np(np.concatenate(own, 0))))
        hs.append(np.stack(split_np(np.concatenate(edge, 0))))
    return np.stack(xs), np.stack(ys), np.stack(hs)


def split(v):
    hi = v.astype(jnp.bfloat16)
    return hi, (v - hi.astype(jnp.float32)).astype(jnp.bfloat16)


def dot(a, b):
    return jnp.dot(a, b, preferred_element_type=jnp.float32)


def kernel(
    gx_n, scale, chunks, per_chunk,
    p_hbm, c_hbm, x_hbm, y_hbm, h_hbm, out_hbm,
    p, c, f, pk, hk, xm, ym, hm, con, ra, rb, ob,
    ld, kd, zs, zr, ds, dr, as_, ar, bs, br, od,
):
    half = p.shape[0]
    rows, cols = p.shape[3], p.shape[4]
    mem, gx, gy = lax.axis_index("mem"), lax.axis_index("gx"), lax.axis_index("gy")
    chip, core = lax.div(mem, 2), lax.rem(mem, 2)
    other = 1 - gy

    def part(k):
        return pl.ds(k * per_chunk, per_chunk)

    def loads(k):
        return [
            pltpu.make_async_copy(src.at[:, :, part(k)], dst.at[:, :, part(k)], ld.at[k, n])
            for n, (src, dst) in enumerate(((p_hbm, p), (c_hbm, c)))
        ]

    def const_loads():
        return [
            pltpu.make_async_copy(x_hbm.at[gx], xm, kd.at[0]),
            pltpu.make_async_copy(y_hbm.at[gy], ym, kd.at[1]),
            pltpu.make_async_copy(h_hbm.at[gy], hm, kd.at[2]),
        ]

    for k in range(chunks):
        for copy in loads(k):
            copy.start()
    for copy in const_loads():
        copy.start()

    barrier = pltpu.get_barrier_semaphore()
    greet = lambda where: pl.semaphore_signal(barrier, inc=1, device_id=where, device_id_type=MESH)
    greet({"gy": other})
    greet({"mem": chip * 2 + 1 - core})
    for k in range(1, half):
        greet({"mem": lax.rem(chip + k, half) * 2 + core})

    @pl.when(gx > 0)
    def _():
        greet({"gx": gx - 1})
        greet({"gx": gx - 1, "gy": other})

    @pl.when(gx < gx_n - 1)
    def _():
        greet({"gx": gx + 1})
        greet({"gx": gx + 1, "gy": other})

    @pl.when(gx == 0)
    def _():
        f[:, :, :, 0:REACH] = jnp.zeros_like(f[:, :, :, 0:REACH])
        hk[:, :, 0:REACH] = jnp.zeros_like(hk[:, :, 0:REACH])

    @pl.when(gx == gx_n - 1)
    def _():
        f[:, :, :, rows + REACH :] = jnp.zeros_like(f[:, :, :, rows + REACH :])
        hk[:, :, rows + REACH :] = jnp.zeros_like(hk[:, :, rows + REACH :])

    pl.semaphore_wait(
        barrier,
        half + 1 + 2 * jnp.where(gx > 0, 1, 0) + 2 * jnp.where(gx < gx_n - 1, 1, 0),
    )

    low, high = pl.ds(0, REACH), pl.ds(rows + REACH, REACH)
    first, last = pl.ds(REACH, REACH), pl.ds(rows, REACH)

    def remote(src, dst, ss, rs, where):
        return pltpu.make_async_remote_copy(
            src_ref=src, dst_ref=dst, send_sem=ss, recv_sem=rs, device_id=where, device_id_type=MESH
        )

    def side(k):
        return remote(
            pk.at[k], hk.at[k, :, pl.ds(REACH, rows)], ds.at[k, 0], dr.at[k, 0], {"gy": other}
        )

    def down(k):
        return (
            remote(f.at[:, :, part(k), first], f.at[:, :, part(k), high], zs.at[k, 0], zr.at[k, 0], {"gx": gx - 1}),
            remote(pk.at[k, :, pl.ds(0, REACH)], hk.at[k, :, high], ds.at[k, 1], dr.at[k, 1], {"gx": gx - 1, "gy": other}),
        )

    def up(k):
        return (
            remote(f.at[:, :, part(k), last], f.at[:, :, part(k), low], zs.at[k, 1], zr.at[k, 1], {"gx": gx + 1}),
            remote(pk.at[k, :, pl.ds(rows - REACH, REACH)], hk.at[k, :, low], ds.at[k, 2], dr.at[k, 2], {"gx": gx + 1, "gy": other}),
        )

    members = [(i, b, j) for j in range(per_chunk) for i in range(half) for b in range(2)]
    groups = [members[n : n + GROUP] for n in range(0, len(members), GROUP)]
    slot = lax.broadcasted_iota(jnp.int32, (rows, LANES), 1) // REACH
    moved = jnp.where(gy == 0, GROUP - 1, 0)

    def send(k, carry):
        for copy in loads(k):
            copy.wait()
        for n, group in enumerate(groups):
            packed = jnp.zeros((rows, LANES), jnp.float32)
            for s, (i, b, j) in enumerate(group):
                at = k * per_chunk + j
                v = p[i, b, at] * c[i, b, at]
                f[i, b, at, pl.ds(REACH, rows)] = v
                edge = jnp.where(gy == 0, v[:, cols - LANES :], v[:, :LANES])
                if s:
                    edge = pltpu.roll(edge, s * REACH, 1)
                packed = jnp.where(slot == lax.rem(s + moved, GROUP), edge, packed)
            pk[k, n] = packed

        @pl.when(gx > 0)
        def _():
            for copy in down(k):
                copy.start()

        @pl.when(gx < gx_n - 1)
        def _():
            for copy in up(k):
                copy.start()

        side(k).start()
        return carry

    lax.fori_loop(0, chunks, send, 0)
    for copy in const_loads():
        copy.wait()

    def to_core(k):
        return remote(
            con.at[:, 1 - core, part(k)], ra.at[:, part(k)], as_.at[k], ar.at[k], {"mem": chip * 2 + 1 - core}
        )

    def to_chip(k, n):
        to = lax.rem(chip + n, half)
        return remote(
            ra.at[to, part(k)], rb.at[n - 1, part(k)], bs.at[k, n - 1], br.at[k, n - 1], {"mem": to * 2 + core}
        )

    def filtered(k):
        @pl.when(gx < gx_n - 1)
        def _():
            for copy in down(k):
                copy.wait_recv()

        @pl.when(gx > 0)
        def _():
            for copy in up(k):
                copy.wait_recv()

        side(k).wait_recv()
        x = xm[...]
        for n, group in enumerate(groups):
            his, los = [], []

            def along_x(v):
                hi, lo = split(v)
                g = dot(x, jnp.concatenate([hi, hi, lo], 0))
                g = jnp.concatenate([g[t * rows : (t + 1) * rows] for t in range(4)], 1)
                return split(g)

            for i, b, j in group:
                hi, lo = along_x(f[i, b, k * per_chunk + j])
                his.append(hi)
                los.append(lo)
            hi, lo = jnp.concatenate(his, 0), jnp.concatenate(los, 0)
            res = dot(hi, ym[0]) + dot(lo, ym[0]) + dot(hi, ym[1])
            hi, lo = along_x(hk[k, n])
            edge = dot(hi, hm[0]) + dot(lo, hm[0]) + dot(hi, hm[1])
            for s, (i, b, j) in enumerate(group):
                at = k * per_chunk + j
                r = res[s * rows : (s + 1) * rows]
                e = pltpu.roll(edge, LANES - s * REACH, 1) if s else edge
                left = jnp.where((slot == 0) & (gy == 1), e, 0.0)
                right = jnp.where((slot == GROUP - 1) & (gy == 0), e, 0.0)
                con[i, b, at, :, :LANES] = p[i, b, at, :, :LANES] * (r[:, :LANES] + left)
                if cols > 2 * LANES:
                    mid = pl.ds(LANES, cols - 2 * LANES)
                    con[i, b, at, :, mid] = p[i, b, at, :, mid] * r[:, LANES : cols - LANES]
                con[i, b, at, :, cols - LANES :] = p[i, b, at, :, cols - LANES :] * (r[:, cols - LANES :] + right)
        to_core(k).start()

    def summed(k):
        to_core(k).wait_recv()
        for n in range(1, half):
            to = lax.rem(chip + n, half)
            ra[to, part(k)] += con[to, core, part(k)]
            to_chip(k, n).start()

    def body(k, carry):
        filtered(k)

        @pl.when(k > 0)
        def _():
            summed(k - 1)

        return carry

    lax.fori_loop(0, chunks, body, 0)
    summed(chunks - 1)

    def finish(k, carry):
        total = con[chip, core, part(k)] + ra[chip, part(k)]
        for n in range(1, half):
            to_chip(k, n).wait_recv()
            total = total + rb[n - 1, part(k)]
        ob[part(k)] = total * scale
        pltpu.make_async_copy(ob.at[part(k)], out_hbm.at[part(k)], od.at[k]).start()
        return carry

    lax.fori_loop(0, chunks, finish, 0)

    def drain(k, carry):
        @pl.when(gx > 0)
        def _():
            for copy in down(k):
                copy.wait_send()

        @pl.when(gx < gx_n - 1)
        def _():
            for copy in up(k):
                copy.wait_send()

        side(k).wait_send()
        to_core(k).wait_send()
        for n in range(1, half):
            to_chip(k, n).wait_send()
        pltpu.make_async_copy(ob.at[part(k)], out_hbm.at[part(k)], od.at[k]).wait()
        return carry

    lax.fori_loop(0, chunks, drain, 0)


def body(perturbations, control):
    mem, gx, gy = (lax.axis_size(a) for a in ("mem", "gx", "gy"))
    members, fields, rows, cols = perturbations.shape
    assert members == 1 and gy == 2 and mem % 2 == 0 and rows >= REACH and cols >= 2 * LANES
    half, per = mem // 2, fields // mem
    per_chunk = next(n for n in range(1, per + 1) if per % n == 0 and mem * n % GROUP == 0)
    chunks = per // per_chunk
    n_groups = mem * per_chunk // GROUP
    xm, ym, hm = constants(rows * gx, cols * gy, gx, gy)
    shape = (half, 2, per, rows, cols)
    tall = rows + 2 * REACH
    f32 = jnp.float32
    any_ = pl.BlockSpec(memory_space=pl.ANY)
    dma = pltpu.SemaphoreType.DMA
    n_to = max(half - 1, 1)
    out = pl.pallas_call(
        functools.partial(kernel, gx, 1.0 / (mem * members - 1), chunks, per_chunk),
        out_shape=jax.ShapeDtypeStruct((per, rows, cols), f32),
        in_specs=[any_] * 5,
        out_specs=any_,
        scratch_shapes=[
            pltpu.VMEM(shape, f32),
            pltpu.VMEM(shape, f32),
            pltpu.VMEM((half, 2, per, tall, cols), f32),
            pltpu.VMEM((chunks, n_groups, rows, LANES), f32),
            pltpu.VMEM((chunks, n_groups, tall, LANES), f32),
            pltpu.VMEM(xm.shape[1:], jnp.bfloat16),
            pltpu.VMEM(ym.shape[1:], jnp.bfloat16),
            pltpu.VMEM(hm.shape[1:], jnp.bfloat16),
            pltpu.VMEM(shape, f32),
            pltpu.VMEM((half, per, rows, cols), f32),
            pltpu.VMEM((n_to, per, rows, cols), f32),
            pltpu.VMEM((per, rows, cols), f32),
            dma((chunks, 2)),
            dma((3,)),
            dma((chunks, 2)),
            dma((chunks, 2)),
            dma((chunks, 3)),
            dma((chunks, 3)),
            dma((chunks,)),
            dma((chunks,)),
            dma((chunks, n_to)),
            dma((chunks, n_to)),
            dma((chunks,)),
        ],
        compiler_params=pltpu.CompilerParams(
            collective_id=0, has_side_effects=True, vmem_limit_bytes=40 * 1024 * 1024
        ),
        cost_estimate=pl.CostEstimate(flops=10**10, bytes_accessed=4 * 2**20, transcendentals=0),
    )(
        perturbations.reshape(shape),
        control.reshape(shape),
        jnp.asarray(xm),
        jnp.asarray(ym),
        jnp.asarray(hm),
    )
    return out


def solution(mesh):
    placed = (P("mem", None, "gx", "gy"), P(None, "gx", "gy"))
    return jax.shard_map(
        body, mesh=mesh, in_specs=placed, out_specs=P("mem", "gx", "gy"), check_vma=False
    )
```

```python
import functools
import math

import jax
import jax.numpy as jnp
import ml_dtypes
import numpy as np
from jax import lax
from jax.experimental import pallas as pl
from jax.experimental.pallas import tpu as pltpu
from jax.sharding import PartitionSpec as P

MESH = pl.DeviceIdType.MESH
REACH = 16
FINE = 8
SENT = 6
GROUP = 8
LANES = 128


def smoothing(n):
    o = np.arange(-4, 5).astype(np.float64)
    taps = np.exp(-o * o / 18.0)
    taps = taps / np.sqrt(np.sum(taps * taps))
    a = np.zeros((n, n))
    for k, t in zip(range(-4, 5), taps):
        a += t * np.eye(n, k=k)
    return a


def factors(n):
    r = np.kron(np.eye(n // 2), np.ones((1, 2))) / math.sqrt(2.0)
    return smoothing(n), smoothing(n // 2), r


def four_terms(n):
    a, small, r = factors(n)
    b = r.T @ small @ r
    return [a @ a, a @ b, b @ a, b @ b]


def split_np(m):
    hi = m.astype(np.float32).astype(ml_dtypes.bfloat16)
    lo = (m - hi.astype(np.float64)).astype(np.float32).astype(ml_dtypes.bfloat16)
    return hi, lo


def triple(m):
    hi, lo = split_np(m)
    return np.concatenate([hi, lo, hi], 1)


def window(m, g, rows, margin):
    wide = np.pad(m, ((0, 0), (margin, margin)))
    return wide[g * rows : (g + 1) * rows, g * rows : (g + 1) * rows + 2 * margin]


def x_constants(nx, gx):
    rows = nx // gx
    crows = rows // 2
    a, small, r = factors(nx)
    terms = four_terms(nx)
    coarse_a = r @ a
    spread = r.T @ small
    main, full, extra, sender = [], [], [], []
    for g in range(gx):
        full.append(triple(np.concatenate([window(m, g, rows, REACH) for m in terms], 0)))
        keep = np.zeros(nx // 2)
        keep[max(0, g * crows - 2) : (g + 1) * crows + 2] = 1.0
        near = [terms[0], terms[1], spread @ (keep[:, None] * coarse_a), terms[3]]
        main.append(triple(np.concatenate([window(m, g, rows, FINE) for m in near], 0)))
        blocks = []
        at_v = [range(g * crows - 8, g * crows - 4), range((g + 1) * crows + 4, (g + 1) * crows + 8)]
        at_w = [range(g * crows - 4, g * crows - 2), range((g + 1) * crows + 2, (g + 1) * crows + 4)]
        for m, is_v in ((a @ spread, True), (r.T @ small @ small, True), (spread, False)):
            e = np.zeros((rows, 16))
            for side in range(2):
                for n, q in enumerate(at_v[side] if is_v else at_w[side]):
                    if 0 <= q < nx // 2:
                        e[:, side * 8 + n + (0 if is_v else 4)] = m[g * rows : (g + 1) * rows, q]
            blocks.append(e)
        extra.append(triple(np.concatenate(blocks, 0)))
        mine = slice(g * rows, (g + 1) * rows)
        s = np.zeros((16, rows))
        low = g * crows
        s[0:4] = r[low + 4 : low + 8, mine]
        s[4:6] = coarse_a[low + 2 : low + 4, mine]
        top = (g + 1) * crows
        s[8:12] = r[top - 8 : top - 4, mine]
        s[12:14] = coarse_a[top - 4 : top - 2, mine]
        sender.append(triple(s))
    return [np.stack(m) for m in (main, full, extra, sender)]


def y_constants(ny, gy):
    cols = ny // gy
    a, small, r = factors(ny)
    extra, sender = [], []
    for g in range(gy):
        mine, coarse = slice(g * cols, (g + 1) * cols), slice(g * cols // 2, (g + 1) * cols // 2)
        parts = [a @ r.T @ small, r.T @ small @ small, r.T]
        extra.append(np.stack(split_np(np.concatenate([m[mine, coarse].T for m in parts], 0))))
        parts = [r, small @ r @ a]
        sender.append(np.stack(split_np(np.concatenate([m[coarse, mine].T for m in parts], 1))))
    return np.stack(extra), np.stack(sender)


def constants(ny, gy):
    cols = ny // gy
    ys, hs = [], []
    for g in range(gy):
        own, edge = [], []
        for m in four_terms(ny):
            mine = m[g * cols : (g + 1) * cols]
            own.append(mine[:, g * cols : (g + 1) * cols].T)
            if g == 0:
                part = mine[cols - REACH :, cols : cols + REACH].T
            else:
                part = mine[:REACH, g * cols - REACH : g * cols].T
            block = np.zeros((LANES, LANES))
            for s in range(GROUP):
                before = (s + GROUP - 1) % GROUP
                slot_in, slot_out = (s, before) if g == 0 else (before, s)
                block[slot_in * REACH :][:REACH, slot_out * REACH : (slot_out + 1) * REACH] = part
            edge.append(block)
        ys.append(np.stack(split_np(np.concatenate(own, 0))))
        hs.append(np.stack(split_np(np.concatenate(edge, 0))))
    return np.stack(ys), np.stack(hs)


def split(v):
    hi = v.astype(jnp.bfloat16)
    return hi, (v - hi.astype(jnp.float32)).astype(jnp.bfloat16)


def dot(a, b):
    return jnp.dot(a, b, preferred_element_type=jnp.float32)


def kernel(
    gx_n, scale, chunks, per_chunk,
    p_hbm, c_hbm, sx_hbm, sy_hbm, x_hbm, xh_hbm, xe_hbm, y_hbm, h_hbm, ye_hbm, out_hbm,
    p, c, f, pk, hk, es, ex, sx, sy, xm, xh, xe, ym, hm, ye, con, ra, rb, ob,
    ld, kd, zs, zr, es_, er, ds, dr, as_, ar, bs, br, od,
):
    half = p.shape[0]
    rows, cols = p.shape[3], p.shape[4]
    mem, gx, gy = lax.axis_index("mem"), lax.axis_index("gx"), lax.axis_index("gy")
    chip, core = lax.div(mem, 2), lax.rem(mem, 2)
    other = 1 - gy

    def part(k):
        return pl.ds(k * per_chunk, per_chunk)

    def loads(k):
        return [
            pltpu.make_async_copy(src.at[:, :, part(k)], dst.at[:, :, part(k)], ld.at[k, n])
            for n, (src, dst) in enumerate(((p_hbm, p), (c_hbm, c)))
        ]

    def const_loads(which):
        pairs = (
            (sx_hbm, sx, gx), (sy_hbm, sy, gy), (x_hbm, xm, gx), (xh_hbm, xh, gx),
            (xe_hbm, xe, gx), (y_hbm, ym, gy), (h_hbm, hm, gy), (ye_hbm, ye, gy),
        )
        return [
            pltpu.make_async_copy(pairs[n][0].at[pairs[n][2]], pairs[n][1], kd.at[n]) for n in which
        ]

    for copy in loads(0) + const_loads((0, 1)):
        copy.start()
    for k in range(1, chunks):
        for copy in loads(k):
            copy.start()
    for copy in const_loads(range(2, 8)):
        copy.start()

    ex[...] = jnp.zeros_like(ex)

    barrier = pltpu.get_barrier_semaphore()
    greet = lambda where: pl.semaphore_signal(barrier, inc=1, device_id=where, device_id_type=MESH)
    greet({"gy": other})
    greet({"mem": chip * 2 + 1 - core})
    for k in range(1, half):
        greet({"mem": lax.rem(chip + k, half) * 2 + core})

    @pl.when(gx > 0)
    def _():
        greet({"gx": gx - 1})
        greet({"gx": gx - 1, "gy": other})

    @pl.when(gx < gx_n - 1)
    def _():
        greet({"gx": gx + 1})
        greet({"gx": gx + 1, "gy": other})

    @pl.when(gx == 0)
    def _():
        f[:, :, :, 0:FINE] = jnp.zeros_like(f[:, :, :, 0:FINE])
        hk[:, :, 0:REACH] = jnp.zeros_like(hk[:, :, 0:REACH])

    @pl.when(gx == gx_n - 1)
    def _():
        f[:, :, :, rows + FINE :] = jnp.zeros_like(f[:, :, :, rows + FINE :])
        hk[:, :, rows + REACH :] = jnp.zeros_like(hk[:, :, rows + REACH :])

    pl.semaphore_wait(
        barrier,
        half + 1 + 2 * jnp.where(gx > 0, 1, 0) + 2 * jnp.where(gx < gx_n - 1, 1, 0),
    )

    low, high = pl.ds(0, REACH), pl.ds(rows + REACH, REACH)
    f_low, f_high = pl.ds(0, FINE), pl.ds(rows + FINE, FINE)
    first, last = pl.ds(FINE, FINE), pl.ds(rows, FINE)
    e_low, e_high = pl.ds(0, SENT), pl.ds(8, SENT)

    def remote(src, dst, ss, rs, where):
        return pltpu.make_async_remote_copy(
            src_ref=src, dst_ref=dst, send_sem=ss, recv_sem=rs, device_id=where, device_id_type=MESH
        )

    def side(k):
        return remote(
            pk.at[k], hk.at[k, :, pl.ds(REACH, rows)], ds.at[k, 0], dr.at[k, 0], {"gy": other}
        )

    def down(k):
        return (
            remote(f.at[:, :, part(k), first], f.at[:, :, part(k), f_high], zs.at[k, 0], zr.at[k, 0], {"gx": gx - 1}),
            remote(es.at[k, :, e_low], ex.at[k, :, e_high], es_.at[k, 0], er.at[k, 0], {"gx": gx - 1}),
            remote(pk.at[k, :, pl.ds(0, REACH)], hk.at[k, :, high], ds.at[k, 1], dr.at[k, 1], {"gx": gx - 1, "gy": other}),
        )

    def up(k):
        return (
            remote(f.at[:, :, part(k), last], f.at[:, :, part(k), f_low], zs.at[k, 1], zr.at[k, 1], {"gx": gx + 1}),
            remote(es.at[k, :, e_high], ex.at[k, :, e_low], es_.at[k, 1], er.at[k, 1], {"gx": gx + 1}),
            remote(pk.at[k, :, pl.ds(rows - REACH, REACH)], hk.at[k, :, low], ds.at[k, 2], dr.at[k, 2], {"gx": gx + 1, "gy": other}),
        )

    members = [(i, b, j) for j in range(per_chunk) for i in range(half) for b in range(2)]
    groups = [members[n : n + GROUP] for n in range(0, len(members), GROUP)]
    slot = lax.broadcasted_iota(jnp.int32, (rows, LANES), 1) // REACH
    moved = jnp.where(gy == 0, GROUP - 1, 0)
    is_v = lax.rem(lax.broadcasted_iota(jnp.int32, (GROUP * 16, cols // 2), 0), 8) < 4

    for copy in const_loads((0, 1)):
        copy.wait()

    def send(k, carry):
        for copy in loads(k):
            copy.wait()
        for n, group in enumerate(groups):
            packed = jnp.zeros((rows, LANES), jnp.float32)
            made = []
            for s, (i, b, j) in enumerate(group):
                at = k * per_chunk + j
                v = p[i, b, at] * c[i, b, at]
                f[i, b, at, pl.ds(FINE, rows)] = v
                hi, lo = split(v)
                made.append(dot(sx[...], jnp.concatenate([hi, hi, lo], 0)))
                edge = jnp.where(gy == 0, v[:, cols - LANES :], v[:, :LANES])
                if s:
                    edge = pltpu.roll(edge, s * REACH, 1)
                packed = jnp.where(slot == lax.rem(s + moved, GROUP), edge, packed)
            pk[k, n] = packed
            hi, lo = split(jnp.concatenate(made, 0))
            made = dot(hi, sy[0]) + dot(lo, sy[0]) + dot(hi, sy[1])
            made = jnp.where(is_v, made[:, : cols // 2], made[:, cols // 2 :])
            for s in range(GROUP):
                es[k, n * GROUP + s] = made[s * 16 : (s + 1) * 16]

        @pl.when(gx > 0)
        def _():
            for copy in down(k):
                copy.start()

        @pl.when(gx < gx_n - 1)
        def _():
            for copy in up(k):
                copy.start()

        side(k).start()
        return carry

    lax.fori_loop(0, chunks, send, 0)
    for copy in const_loads(range(2, 8)):
        copy.wait()

    def to_core(k):
        return remote(
            con.at[:, 1 - core, part(k)], ra.at[:, part(k)], as_.at[k], ar.at[k], {"mem": chip * 2 + 1 - core}
        )

    def to_chip(k, n):
        to = lax.rem(chip + n, half)
        return remote(
            ra.at[to, part(k)], rb.at[n - 1, part(k)], bs.at[k, n - 1], br.at[k, n - 1], {"mem": to * 2 + core}
        )

    def filtered(k):
        @pl.when(gx < gx_n - 1)
        def _():
            for copy in down(k):
                copy.wait_recv()

        @pl.when(gx > 0)
        def _():
            for copy in up(k):
                copy.wait_recv()

        side(k).wait_recv()
        for n, group in enumerate(groups):
            his, los, ehis, elos = [], [], [], []

            def along_x(m, v):
                hi, lo = split(v)
                g = dot(m, jnp.concatenate([hi, hi, lo], 0))
                terms = m.shape[0] // rows
                g = jnp.concatenate([g[t * rows : (t + 1) * rows] for t in range(terms)], 1)
                return split(g)

            for s, (i, b, j) in enumerate(group):
                hi, lo = along_x(xm[...], f[i, b, k * per_chunk + j])
                his.append(hi)
                los.append(lo)
                hi, lo = along_x(xe[...], ex[k, n * GROUP + s])
                ehis.append(hi)
                elos.append(lo)
            hi, lo = jnp.concatenate(his, 0), jnp.concatenate(los, 0)
            res = dot(hi, ym[0]) + dot(lo, ym[0]) + dot(hi, ym[1])
            hi, lo = jnp.concatenate(ehis, 0), jnp.concatenate(elos, 0)
            res = res + (dot(hi, ye[0]) + dot(lo, ye[0]) + dot(hi, ye[1]))
            hi, lo = along_x(xh[...], hk[k, n])
            edge = dot(hi, hm[0]) + dot(lo, hm[0]) + dot(hi, hm[1])
            for s, (i, b, j) in enumerate(group):
                at = k * per_chunk + j
                r = res[s * rows : (s + 1) * rows]
                e = pltpu.roll(edge, LANES - s * REACH, 1) if s else edge
                left = jnp.where((slot == 0) & (gy == 1), e, 0.0)
                right = jnp.where((slot == GROUP - 1) & (gy == 0), e, 0.0)
                con[i, b, at, :, :LANES] = p[i, b, at, :, :LANES] * (r[:, :LANES] + left)
                if cols > 2 * LANES:
                    mid = pl.ds(LANES, cols - 2 * LANES)
                    con[i, b, at, :, mid] = p[i, b, at, :, mid] * r[:, LANES : cols - LANES]
                con[i, b, at, :, cols - LANES :] = p[i, b, at, :, cols - LANES :] * (r[:, cols - LANES :] + right)
        to_core(k).start()

    def summed(k):
        to_core(k).wait_recv()
        for n in range(1, half):
            to = lax.rem(chip + n, half)
            ra[to, part(k)] += con[to, core, part(k)]
            to_chip(k, n).start()

    def body(k, carry):
        filtered(k)

        @pl.when(k > 0)
        def _():
            summed(k - 1)

        return carry

    lax.fori_loop(0, chunks, body, 0)
    summed(chunks - 1)

    def finish(k, carry):
        total = con[chip, core, part(k)] + ra[chip, part(k)]
        for n in range(1, half):
            to_chip(k, n).wait_recv()
            total = total + rb[n - 1, part(k)]
        ob[part(k)] = total * scale
        pltpu.make_async_copy(ob.at[part(k)], out_hbm.at[part(k)], od.at[k]).start()
        return carry

    lax.fori_loop(0, chunks, finish, 0)

    def drain(k, carry):
        @pl.when(gx > 0)
        def _():
            for copy in down(k):
                copy.wait_send()

        @pl.when(gx < gx_n - 1)
        def _():
            for copy in up(k):
                copy.wait_send()

        side(k).wait_send()
        to_core(k).wait_send()
        for n in range(1, half):
            to_chip(k, n).wait_send()
        pltpu.make_async_copy(ob.at[part(k)], out_hbm.at[part(k)], od.at[k]).wait()
        return carry

    lax.fori_loop(0, chunks, drain, 0)


def body(perturbations, control):
    mem, gx, gy = (lax.axis_size(a) for a in ("mem", "gx", "gy"))
    members, fields, rows, cols = perturbations.shape
    assert members == 1 and gy == 2 and mem % 2 == 0 and rows >= REACH and cols >= 2 * LANES
    half, per = mem // 2, fields // mem
    per_chunk = next(n for n in range(1, per + 1) if per % n == 0 and mem * n % GROUP == 0)
    chunks = per // per_chunk
    n_groups = mem * per_chunk // GROUP
    xm, xh, xe, sx = x_constants(rows * gx, gx)
    ym, hm = constants(cols * gy, gy)
    ye, sy = y_constants(cols * gy, gy)
    fixed = (sx, sy, xm, xh, xe, ym, hm, ye)
    shape = (half, 2, per, rows, cols)
    tall = rows + 2 * REACH
    f32 = jnp.float32
    any_ = pl.BlockSpec(memory_space=pl.ANY)
    dma = pltpu.SemaphoreType.DMA
    n_to = max(half - 1, 1)
    out = pl.pallas_call(
        functools.partial(kernel, gx, 1.0 / (mem * members - 1), chunks, per_chunk),
        out_shape=jax.ShapeDtypeStruct((per, rows, cols), f32),
        in_specs=[any_] * (2 + len(fixed)),
        out_specs=any_,
        scratch_shapes=[
            pltpu.VMEM(shape, f32),
            pltpu.VMEM(shape, f32),
            pltpu.VMEM((half, 2, per, rows + 2 * FINE, cols), f32),
            pltpu.VMEM((chunks, n_groups, rows, LANES), f32),
            pltpu.VMEM((chunks, n_groups, tall, LANES), f32),
            pltpu.VMEM((chunks, n_groups * GROUP, 16, cols // 2), f32),
            pltpu.VMEM((chunks, n_groups * GROUP, 16, cols // 2), f32),
            *[pltpu.VMEM(m.shape[1:], jnp.bfloat16) for m in fixed],
            pltpu.VMEM(shape, f32),
            pltpu.VMEM((half, per, rows, cols), f32),
            pltpu.VMEM((n_to, per, rows, cols), f32),
            pltpu.VMEM((per, rows, cols), f32),
            dma((chunks, 2)),
            dma((len(fixed),)),
            dma((chunks, 2)),
            dma((chunks, 2)),
            dma((chunks, 2)),
            dma((chunks, 2)),
            dma((chunks, 3)),
            dma((chunks, 3)),
            dma((chunks,)),
            dma((chunks,)),
            dma((chunks, n_to)),
            dma((chunks, n_to)),
            dma((chunks,)),
        ],
        compiler_params=pltpu.CompilerParams(
            collective_id=0, has_side_effects=True, vmem_limit_bytes=63 * 1024 * 1024
        ),
        cost_estimate=pl.CostEstimate(flops=10**10, bytes_accessed=4 * 2**20, transcendentals=0),
    )(
        perturbations.reshape(shape),
        control.reshape(shape),
        *[jnp.asarray(m) for m in fixed],
    )
    return out


def solution(mesh):
    placed = (P("mem", None, "gx", "gy"), P(None, "gx", "gy"))
    return jax.shard_map(
        body, mesh=mesh, in_specs=placed, out_specs=P("mem", "gx", "gy"), check_vma=False
    )
```

```python
import functools
import math

import jax
import jax.numpy as jnp
import ml_dtypes
import numpy as np
from jax import lax
from jax.experimental import pallas as pl
from jax.experimental.pallas import tpu as pltpu
from jax.sharding import PartitionSpec as P

MESH = pl.DeviceIdType.MESH
REACH = 16
FINE = 8
SENT = 6
GROUP = 8
LANES = 128


def smoothing(n):
    o = np.arange(-4, 5).astype(np.float64)
    taps = np.exp(-o * o / 18.0)
    taps = taps / np.sqrt(np.sum(taps * taps))
    a = np.zeros((n, n))
    for k, t in zip(range(-4, 5), taps):
        a += t * np.eye(n, k=k)
    return a


def factors(n):
    r = np.kron(np.eye(n // 2), np.ones((1, 2))) / math.sqrt(2.0)
    return smoothing(n), smoothing(n // 2), r


def four_terms(n):
    a, small, r = factors(n)
    b = r.T @ small @ r
    return [a @ a, a @ b, b @ a, b @ b]


def split_np(m):
    hi = m.astype(np.float32).astype(ml_dtypes.bfloat16)
    lo = (m - hi.astype(np.float64)).astype(np.float32).astype(ml_dtypes.bfloat16)
    return hi, lo


def triple(m):
    hi, lo = split_np(m)
    return np.concatenate([hi, lo, hi], 1)


def window(m, g, rows, margin):
    wide = np.pad(m, ((0, 0), (margin, margin)))
    return wide[g * rows : (g + 1) * rows, g * rows : (g + 1) * rows + 2 * margin]


def x_constants(nx, gx):
    rows = nx // gx
    crows = rows // 2
    a, small, r = factors(nx)
    terms = four_terms(nx)
    coarse_a = r @ a
    spread = r.T @ small
    main, full, extra, sender = [], [], [], []
    for g in range(gx):
        full.append(triple(np.concatenate([window(m, g, rows, REACH) for m in terms], 0)))
        keep = np.zeros(nx // 2)
        keep[max(0, g * crows - 2) : (g + 1) * crows + 2] = 1.0
        near = [terms[0], terms[1], spread @ (keep[:, None] * coarse_a), terms[3]]
        main.append(triple(np.concatenate([window(m, g, rows, FINE) for m in near], 0)))
        blocks = []
        at_v = [range(g * crows - 8, g * crows - 4), range((g + 1) * crows + 4, (g + 1) * crows + 8)]
        at_w = [range(g * crows - 4, g * crows - 2), range((g + 1) * crows + 2, (g + 1) * crows + 4)]
        for m, is_v in ((a @ spread, True), (r.T @ small @ small, True), (spread, False)):
            e = np.zeros((rows, 16))
            for side in range(2):
                for n, q in enumerate(at_v[side] if is_v else at_w[side]):
                    if 0 <= q < nx // 2:
                        e[:, side * 8 + n + (0 if is_v else 4)] = m[g * rows : (g + 1) * rows, q]
            blocks.append(e)
        extra.append(triple(np.concatenate(blocks, 0)))
        mine = slice(g * rows, (g + 1) * rows)
        s = np.zeros((16, rows))
        low = g * crows
        s[0:4] = r[low + 4 : low + 8, mine]
        s[4:6] = coarse_a[low + 2 : low + 4, mine]
        top = (g + 1) * crows
        s[8:12] = r[top - 8 : top - 4, mine]
        s[12:14] = coarse_a[top - 4 : top - 2, mine]
        sender.append(triple(s))
    return [np.stack(m) for m in (main, full, extra, sender)]


def y_constants(ny, gy):
    cols = ny // gy
    a, small, r = factors(ny)
    extra, sender = [], []
    for g in range(gy):
        mine, coarse = slice(g * cols, (g + 1) * cols), slice(g * cols // 2, (g + 1) * cols // 2)
        parts = [a @ r.T @ small, r.T @ small @ small, r.T]
        extra.append(np.stack(split_np(np.concatenate([m[mine, coarse].T for m in parts], 0))))
        parts = [r, small @ r @ a]
        sender.append(np.stack(split_np(np.concatenate([m[coarse, mine].T for m in parts], 1))))
    return np.stack(extra), np.stack(sender)


def constants(ny, gy):
    cols = ny // gy
    ys, hs = [], []
    for g in range(gy):
        own, edge = [], []
        for m in four_terms(ny):
            mine = m[g * cols : (g + 1) * cols]
            own.append(mine[:, g * cols : (g + 1) * cols].T)
            if g == 0:
                part = mine[cols - REACH :, cols : cols + REACH].T
            else:
                part = mine[:REACH, g * cols - REACH : g * cols].T
            block = np.zeros((LANES, LANES))
            for s in range(GROUP):
                before = (s + GROUP - 1) % GROUP
                slot_in, slot_out = (s, before) if g == 0 else (before, s)
                block[slot_in * REACH :][:REACH, slot_out * REACH : (slot_out + 1) * REACH] = part
            edge.append(block)
        ys.append(np.stack(split_np(np.concatenate(own, 0))))
        hs.append(np.stack(split_np(np.concatenate(edge, 0))))
    return np.stack(ys), np.stack(hs)


def split(v):
    hi = v.astype(jnp.bfloat16)
    return hi, (v - hi.astype(jnp.float32)).astype(jnp.bfloat16)


def dot(a, b):
    return jnp.dot(a, b, preferred_element_type=jnp.float32)


def kernel(
    gx_n, scale, chunks, per_chunk,
    p_hbm, c_hbm, sx_hbm, sy_hbm, x_hbm, xh_hbm, xe_hbm, y_hbm, h_hbm, ye_hbm, out_hbm,
    p, c, f, pk, hk, es, ex, sx, sy, xm, xh, xe, ym, hm, ye, con, ra, rb, ob,
    ld, kd, zs, zr, es_, er, ds, dr, as_, ar, bs, br, od,
):
    half = p.shape[0]
    rows, cols = p.shape[3], p.shape[4]
    mem, gx, gy = lax.axis_index("mem"), lax.axis_index("gx"), lax.axis_index("gy")
    chip, core = lax.div(mem, 2), lax.rem(mem, 2)
    other = 1 - gy

    def part(k):
        return pl.ds(k * per_chunk, per_chunk)

    def loads(k):
        return [
            pltpu.make_async_copy(src.at[:, :, part(k)], dst.at[:, :, part(k)], ld.at[k, n])
            for n, (src, dst) in enumerate(((p_hbm, p), (c_hbm, c)))
        ]

    def const_loads(which):
        pairs = (
            (sx_hbm, sx, gx), (sy_hbm, sy, gy), (x_hbm, xm, gx), (xh_hbm, xh, gx),
            (xe_hbm, xe, gx), (y_hbm, ym, gy), (h_hbm, hm, gy), (ye_hbm, ye, gy),
        )
        return [
            pltpu.make_async_copy(pairs[n][0].at[pairs[n][2]], pairs[n][1], kd.at[n]) for n in which
        ]

    for copy in loads(0) + const_loads((0, 1)):
        copy.start()
    for k in range(1, chunks):
        for copy in loads(k):
            copy.start()
    for copy in const_loads(range(2, 8)):
        copy.start()

    ex[...] = jnp.zeros_like(ex)

    barrier = pltpu.get_barrier_semaphore()
    greet = lambda where: pl.semaphore_signal(barrier, inc=1, device_id=where, device_id_type=MESH)
    greet({"gy": other})
    greet({"mem": chip * 2 + 1 - core})
    for k in range(1, half):
        greet({"mem": lax.rem(chip + k, half) * 2 + core})

    @pl.when(gx > 0)
    def _():
        greet({"gx": gx - 1})
        greet({"gx": gx - 1, "gy": other})

    @pl.when(gx < gx_n - 1)
    def _():
        greet({"gx": gx + 1})
        greet({"gx": gx + 1, "gy": other})

    @pl.when(gx == 0)
    def _():
        f[:, :, :, 0:FINE] = jnp.zeros_like(f[:, :, :, 0:FINE])
        hk[:, :, 0:REACH] = jnp.zeros_like(hk[:, :, 0:REACH])

    @pl.when(gx == gx_n - 1)
    def _():
        f[:, :, :, rows + FINE :] = jnp.zeros_like(f[:, :, :, rows + FINE :])
        hk[:, :, rows + REACH :] = jnp.zeros_like(hk[:, :, rows + REACH :])

    pl.semaphore_wait(
        barrier,
        half + 1 + 2 * jnp.where(gx > 0, 1, 0) + 2 * jnp.where(gx < gx_n - 1, 1, 0),
    )

    low, high = pl.ds(0, REACH), pl.ds(rows + REACH, REACH)
    f_low, f_high = pl.ds(0, FINE), pl.ds(rows + FINE, FINE)
    first, last = pl.ds(FINE, FINE), pl.ds(rows, FINE)
    e_low, e_high = pl.ds(0, SENT), pl.ds(8, SENT)

    def remote(src, dst, ss, rs, where):
        return pltpu.make_async_remote_copy(
            src_ref=src, dst_ref=dst, send_sem=ss, recv_sem=rs, device_id=where, device_id_type=MESH
        )

    def side(k):
        return remote(
            pk.at[k], hk.at[k, :, pl.ds(REACH, rows)], ds.at[k, 0], dr.at[k, 0], {"gy": other}
        )

    def down(k):
        return (
            remote(f.at[:, :, part(k), first], f.at[:, :, part(k), f_high], zs.at[k, 0], zr.at[k, 0], {"gx": gx - 1}),
            remote(es.at[k, :, e_low], ex.at[k, :, e_high], es_.at[k, 0], er.at[k, 0], {"gx": gx - 1}),
            remote(pk.at[k, :, pl.ds(0, REACH)], hk.at[k, :, high], ds.at[k, 1], dr.at[k, 1], {"gx": gx - 1, "gy": other}),
        )

    def up(k):
        return (
            remote(f.at[:, :, part(k), last], f.at[:, :, part(k), f_low], zs.at[k, 1], zr.at[k, 1], {"gx": gx + 1}),
            remote(es.at[k, :, e_high], ex.at[k, :, e_low], es_.at[k, 1], er.at[k, 1], {"gx": gx + 1}),
            remote(pk.at[k, :, pl.ds(rows - REACH, REACH)], hk.at[k, :, low], ds.at[k, 2], dr.at[k, 2], {"gx": gx + 1, "gy": other}),
        )

    members = [(i, b, j) for j in range(per_chunk) for i in range(half) for b in range(2)]
    groups = [members[n : n + GROUP] for n in range(0, len(members), GROUP)]
    slot = lax.broadcasted_iota(jnp.int32, (rows, LANES), 1) // REACH
    moved = jnp.where(gy == 0, GROUP - 1, 0)
    is_v = lax.rem(lax.broadcasted_iota(jnp.int32, (GROUP * 16, cols // 2), 0), 8) < 4

    for copy in const_loads((0, 1)):
        copy.wait()

    def start(k, which):
        @pl.when(gx > 0)
        def _():
            for n in which:
                down(k)[n].start()

        @pl.when(gx < gx_n - 1)
        def _():
            for n in which:
                up(k)[n].start()

    def send(k, carry):
        for copy in loads(k):
            copy.wait()
        for n, group in enumerate(groups):
            packed = jnp.zeros((rows, LANES), jnp.float32)
            for s, (i, b, j) in enumerate(group):
                at = k * per_chunk + j
                v = p[i, b, at] * c[i, b, at]
                f[i, b, at, pl.ds(FINE, rows)] = v
                edge = jnp.where(gy == 0, v[:, cols - LANES :], v[:, :LANES])
                if s:
                    edge = pltpu.roll(edge, s * REACH, 1)
                packed = jnp.where(slot == lax.rem(s + moved, GROUP), edge, packed)
            pk[k, n] = packed

        start(k, (0, 2))
        side(k).start()
        for n, group in enumerate(groups):
            made = []
            for i, b, j in group:
                hi, lo = split(f[i, b, k * per_chunk + j, pl.ds(FINE, rows)])
                made.append(dot(sx[...], jnp.concatenate([hi, hi, lo], 0)))
            hi, lo = split(jnp.concatenate(made, 0))
            made = dot(hi, sy[0]) + dot(lo, sy[0]) + dot(hi, sy[1])
            made = jnp.where(is_v, made[:, : cols // 2], made[:, cols // 2 :])
            for s in range(len(group)):
                es[k, n * GROUP + s] = made[s * 16 : (s + 1) * 16]
        start(k, (1,))
        return carry

    lax.fori_loop(0, chunks, send, 0)
    for copy in const_loads(range(2, 8)):
        copy.wait()

    def to_core(k):
        return remote(
            con.at[:, 1 - core, part(k)], ra.at[:, part(k)], as_.at[k], ar.at[k], {"mem": chip * 2 + 1 - core}
        )

    def to_chip(k, n):
        to = lax.rem(chip + n, half)
        return remote(
            ra.at[to, part(k)], rb.at[n - 1, part(k)], bs.at[k, n - 1], br.at[k, n - 1], {"mem": to * 2 + core}
        )

    def filtered(k):
        @pl.when(gx < gx_n - 1)
        def _():
            for copy in down(k):
                copy.wait_recv()

        @pl.when(gx > 0)
        def _():
            for copy in up(k):
                copy.wait_recv()

        side(k).wait_recv()
        for n, group in enumerate(groups):
            his, los, ehis, elos = [], [], [], []

            def along_x(m, v):
                hi, lo = split(v)
                g = dot(m, jnp.concatenate([hi, hi, lo], 0))
                terms = m.shape[0] // rows
                g = jnp.concatenate([g[t * rows : (t + 1) * rows] for t in range(terms)], 1)
                return split(g)

            for s, (i, b, j) in enumerate(group):
                hi, lo = along_x(xm[...], f[i, b, k * per_chunk + j])
                his.append(hi)
                los.append(lo)
                hi, lo = along_x(xe[...], ex[k, n * GROUP + s])
                ehis.append(hi)
                elos.append(lo)
            hi, lo = jnp.concatenate(his, 0), jnp.concatenate(los, 0)
            res = dot(hi, ym[0]) + dot(lo, ym[0]) + dot(hi, ym[1])
            hi, lo = jnp.concatenate(ehis, 0), jnp.concatenate(elos, 0)
            res = res + (dot(hi, ye[0]) + dot(lo, ye[0]) + dot(hi, ye[1]))
            hi, lo = along_x(xh[...], hk[k, n])
            edge = dot(hi, hm[0]) + dot(lo, hm[0]) + dot(hi, hm[1])
            for s, (i, b, j) in enumerate(group):
                at = k * per_chunk + j
                r = res[s * rows : (s + 1) * rows]
                e = pltpu.roll(edge, LANES - s * REACH, 1) if s else edge
                left = jnp.where((slot == 0) & (gy == 1), e, 0.0)
                right = jnp.where((slot == GROUP - 1) & (gy == 0), e, 0.0)
                con[i, b, at, :, :LANES] = p[i, b, at, :, :LANES] * (r[:, :LANES] + left)
                if cols > 2 * LANES:
                    mid = pl.ds(LANES, cols - 2 * LANES)
                    con[i, b, at, :, mid] = p[i, b, at, :, mid] * r[:, LANES : cols - LANES]
                con[i, b, at, :, cols - LANES :] = p[i, b, at, :, cols - LANES :] * (r[:, cols - LANES :] + right)
        to_core(k).start()

    def summed(k):
        to_core(k).wait_recv()
        for n in range(1, half):
            to = lax.rem(chip + n, half)
            ra[to, part(k)] += con[to, core, part(k)]
            to_chip(k, n).start()

    def body(k, carry):
        filtered(k)

        @pl.when(k > 0)
        def _():
            summed(k - 1)

        return carry

    lax.fori_loop(0, chunks, body, 0)
    summed(chunks - 1)

    def finish(k, carry):
        total = con[chip, core, part(k)] + ra[chip, part(k)]
        for n in range(1, half):
            to_chip(k, n).wait_recv()
            total = total + rb[n - 1, part(k)]
        ob[part(k)] = total * scale
        pltpu.make_async_copy(ob.at[part(k)], out_hbm.at[part(k)], od.at[k]).start()
        return carry

    lax.fori_loop(0, chunks, finish, 0)

    def drain(k, carry):
        @pl.when(gx > 0)
        def _():
            for copy in down(k):
                copy.wait_send()

        @pl.when(gx < gx_n - 1)
        def _():
            for copy in up(k):
                copy.wait_send()

        side(k).wait_send()
        to_core(k).wait_send()
        for n in range(1, half):
            to_chip(k, n).wait_send()
        pltpu.make_async_copy(ob.at[part(k)], out_hbm.at[part(k)], od.at[k]).wait()
        return carry

    lax.fori_loop(0, chunks, drain, 0)


def body(perturbations, control):
    mem, gx, gy = (lax.axis_size(a) for a in ("mem", "gx", "gy"))
    members, fields, rows, cols = perturbations.shape
    assert members == 1 and gy == 2 and mem % 2 == 0 and rows >= REACH and cols >= 2 * LANES
    half, per = mem // 2, fields // mem
    per_chunk = next(n for n in range(1, per + 1) if per % n == 0 and mem * n % GROUP == 0)
    chunks = per // per_chunk
    n_groups = mem * per_chunk // GROUP
    xm, xh, xe, sx = x_constants(rows * gx, gx)
    ym, hm = constants(cols * gy, gy)
    ye, sy = y_constants(cols * gy, gy)
    fixed = (sx, sy, xm, xh, xe, ym, hm, ye)
    shape = (half, 2, per, rows, cols)
    tall = rows + 2 * REACH
    f32 = jnp.float32
    any_ = pl.BlockSpec(memory_space=pl.ANY)
    dma = pltpu.SemaphoreType.DMA
    n_to = max(half - 1, 1)
    out = pl.pallas_call(
        functools.partial(kernel, gx, 1.0 / (mem * members - 1), chunks, per_chunk),
        out_shape=jax.ShapeDtypeStruct((per, rows, cols), f32),
        in_specs=[any_] * (2 + len(fixed)),
        out_specs=any_,
        scratch_shapes=[
            pltpu.VMEM(shape, f32),
            pltpu.VMEM(shape, f32),
            pltpu.VMEM((half, 2, per, rows + 2 * FINE, cols), f32),
            pltpu.VMEM((chunks, n_groups, rows, LANES), f32),
            pltpu.VMEM((chunks, n_groups, tall, LANES), f32),
            pltpu.VMEM((chunks, n_groups * GROUP, 16, cols // 2), f32),
            pltpu.VMEM((chunks, n_groups * GROUP, 16, cols // 2), f32),
            *[pltpu.VMEM(m.shape[1:], jnp.bfloat16) for m in fixed],
            pltpu.VMEM(shape, f32),
            pltpu.VMEM((half, per, rows, cols), f32),
            pltpu.VMEM((n_to, per, rows, cols), f32),
            pltpu.VMEM((per, rows, cols), f32),
            dma((chunks, 2)),
            dma((len(fixed),)),
            dma((chunks, 2)),
            dma((chunks, 2)),
            dma((chunks, 2)),
            dma((chunks, 2)),
            dma((chunks, 3)),
            dma((chunks, 3)),
            dma((chunks,)),
            dma((chunks,)),
            dma((chunks, n_to)),
            dma((chunks, n_to)),
            dma((chunks,)),
        ],
        compiler_params=pltpu.CompilerParams(
            collective_id=0, has_side_effects=True, vmem_limit_bytes=63 * 1024 * 1024
        ),
        cost_estimate=pl.CostEstimate(flops=10**10, bytes_accessed=4 * 2**20, transcendentals=0),
    )(
        perturbations.reshape(shape),
        control.reshape(shape),
        *[jnp.asarray(m) for m in fixed],
    )
    return out


def solution(mesh):
    placed = (P("mem", None, "gx", "gy"), P(None, "gx", "gy"))
    return jax.shard_map(
        body, mesh=mesh, in_specs=placed, out_specs=P("mem", "gx", "gy"), check_vma=False
    )
```
